32 devices in a mesh: grid: 8 (over z, x), kpt: 4 (over y, core).
Axes of the slice: x: 2, y: 2, z: 4, core: 2. Of those that a mesh axis runs over, the one named last changes fastest.
Arguments:
- orbitals: bfloat16 [256, 13, 48, 128], P(('grid', 'kpt')), may hold values from -0.19921875 to 0.19921875
- potential: float32 [256, 128], P(('grid', 'kpt')), may hold values from -3 to 1
- batch_pairs: int32 [256, 48, 48], P(('grid', 'kpt')), may hold values from 0 to 255, as said below
- pair_info: int32 [3, 256], replicated, may hold values from 0 to 60, as said below
- mirror: int32 [256], replicated, may hold values from 0 to 255, as said below
- cell_table: int32 [61, 3], replicated, may hold values from -3 to 3, as said below
- kpoints: float32 [4, 3], P('kpt'), may hold values from -0.5 to 0.5
Outputs:
- hamiltonian: float32 [4, 2, 32, 13, 416], P('kpt', None, 'grid')
The draws below stay inside these ranges and needn't reach their ends.
Inputs may be any that keep to these rules, and one draw needn't show every extreme that they name: Pair n = (g * 4 + c) * 8 + q belongs to grid index g and kpt index c, and its first atom pair_info[0, n] lies in q * 4 to (q + 1) * 4 - 1; pair_info[2, n] is a cell index below 61. mirror is an involution without fixed points; mirror[n] has first atom pair_info[1, n], second atom pair_info[0, n] and cell 61 - 1 - pair_info[2, n]; the mirror of a pair of grid index g and kpt index c belongs to grid index (g + 4) mod 8 and the same kpt index. cell_table[60 - r] = -cell_table[r]; the middle cell is the zero vector. `batch_pairs`: A batch held by grid index g and kpt index c names only pairs of kpt index c and of grid index g - 1, g or g + 1 (mod 8).
All inputs are finite; a program needn't handle non-finite values.
Results may differ from the reference program's by a relative error of at most 0.00093.
Values sent between devices are 32-bit elements; how exact they have to be, the bound alone decides.
A program may use at most 128 MiB of HBM per device.

```python
import math
import jax
import jax.numpy as jnp
from jax import lax

NAO = 13
NCELL = 61
ABAT = 48
PTS = 128
BAT_DEV = 8
ATOM_DEV = 4
ROWPAIRS = 1
ATOMS = 32
PAIR_DEV = 8
NPAIR = 256
BATCHES = 256
NK = 4
N_GRID = 8
N_KPT = 4


def pair_world(key):
    half = N_GRID // 2
    base = jax.random.fold_in(key, 11)
    key_perm, key_first, key_second, key_cell = jax.random.split(base, 4)
    slots = jnp.arange(PAIR_DEV, dtype=jnp.int32)
    perm_keys = jax.random.split(key_perm, half * N_KPT)
    shuffles = jax.vmap(lambda one_key: jax.random.permutation(one_key, PAIR_DEV))(perm_keys)
    shuffles = shuffles.reshape(half, N_KPT, PAIR_DEV).astype(jnp.int32)
    owner_first = (slots // ROWPAIRS)[None, None, :]
    owner_second = shuffles // ROWPAIRS
    first_atom = owner_first * ATOM_DEV + jax.random.randint(key_first, (half, N_KPT, PAIR_DEV), 0, ATOM_DEV).astype(jnp.int32)
    second_atom = owner_second * ATOM_DEV + jax.random.randint(key_second, (half, N_KPT, PAIR_DEV), 0, ATOM_DEV).astype(jnp.int32)
    cell_index = jax.random.randint(key_cell, (half, N_KPT, PAIR_DEV), 0, NCELL).astype(jnp.int32)
    grid_low = jnp.arange(half, dtype=jnp.int32)[:, None, None]
    kpt_all = jnp.arange(N_KPT, dtype=jnp.int32)[None, :, None]
    low_ids = ((grid_low * N_KPT + kpt_all) * PAIR_DEV + slots[None, None, :]).reshape(-1)
    high_ids = (((grid_low + half) * N_KPT + kpt_all) * PAIR_DEV + shuffles).reshape(-1)
    first_atom = first_atom.reshape(-1)
    second_atom = second_atom.reshape(-1)
    cell_index = cell_index.reshape(-1)
    blank = jnp.zeros((NPAIR,), jnp.int32)
    info_first = blank.at[low_ids].set(first_atom).at[high_ids].set(second_atom)
    info_second = blank.at[low_ids].set(second_atom).at[high_ids].set(first_atom)
    info_cell = blank.at[low_ids].set(cell_index).at[high_ids].set(NCELL - 1 - cell_index)
    partner = blank.at[low_ids].set(high_ids).at[high_ids].set(low_ids)
    return (jnp.stack([info_first, info_second, info_cell]), partner)


def draw_pair_info(key, part):
    return pair_world(key)[0]


def draw_mirror(key, part):
    return pair_world(key)[1]


def draw_cell_table(key, part):
    half = (NCELL - 1) // 2
    lower = jax.random.randint(jax.random.fold_in(key, 3), (half, 3), -3, 4).astype(jnp.int32)
    return jnp.concatenate([lower, jnp.zeros((1, 3), jnp.int32), -lower[::-1]], axis=0)


def draw_batch_pairs(key, part):
    key_step, key_slot = jax.random.split(jax.random.fold_in(key, 23), 2)
    batch = jnp.arange(BATCHES, dtype=jnp.int32)
    device = batch // BAT_DEV
    grid_pos = (device // N_KPT)[:, None, None]
    kpt_pos = (device % N_KPT)[:, None, None]
    step = jax.random.randint(key_step, (BATCHES, ABAT, ABAT), -1, 2).astype(jnp.int32)
    slot = jax.random.randint(key_slot, (BATCHES, ABAT, ABAT), 0, PAIR_DEV).astype(jnp.int32)
    holder = (grid_pos + step + N_GRID) % N_GRID
    ids = (holder * N_KPT + kpt_pos) * PAIR_DEV + slot
    first = (device // N_KPT * N_KPT + device % N_KPT) * PAIR_DEV
    ids = ids.at[:, 0, 0].set(first).at[:, 1, 1].set(first + PAIR_DEV - 1)
    return ids.astype(jnp.int32)


def steps_of(rng, dims, cuts, least, top_value):
    factor_of = 1.0
    for axis_at, blocks in cuts:
        steps = jax.random.uniform(jax.random.fold_in(jax.random.fold_in(rng, 6), axis_at), (blocks,), jnp.float32, least / len(cuts), top_value / len(cuts))
        factor_of = factor_of * jnp.repeat(jnp.exp(steps), dims[axis_at] // blocks).reshape((-1,) + (1,) * (len(dims) - 1 - axis_at))
    return factor_of


def bell_draw(own_key, extent, width, most, shards=(), held_as=jnp.bfloat16):
    array = jax.random.normal(own_key, extent, jnp.float32) * width
    if len(shards) > 0:
        array = steps_of(own_key, extent, shards, -0.22, 0.18) * array
    return jnp.clip(array, min=-most, max=most).astype(held_as)


def setup_inputs(seed: int = 0) -> dict:
    streams_of = jax.random.split(jax.random.key(seed), 8)
    orbitals = bell_draw(streams_of[0], (BATCHES, NAO, ABAT, PTS), 0.035, 0.19921875, ((0, 32),))
    potential = jnp.clip(-3.0 + 4.0 * jax.random.uniform(streams_of[1], (BATCHES, PTS), jnp.float32) ** steps_of(streams_of[1], (BATCHES, PTS), ((0, 32),), -0.2, 0.2), -3.0, 1.0)
    batch_pairs = draw_batch_pairs(jax.random.fold_in(streams_of[7], 71), 0)
    pair_info = draw_pair_info(jax.random.fold_in(streams_of[7], 71), 0)
    mirror = draw_mirror(jax.random.fold_in(streams_of[7], 71), 0)
    cell_table = draw_cell_table(jax.random.fold_in(streams_of[7], 71), 0)
    kpoints = jnp.clip(jax.random.uniform(streams_of[6], (NK, 3), jnp.float32, -0.5, 0.5) * steps_of(streams_of[6], (NK, 3), ((0, 4),), -0.4, 0.0), -0.5, 0.5)
    return dict(orbitals=orbitals, potential=potential, batch_pairs=batch_pairs, pair_info=pair_info, mirror=mirror, cell_table=cell_table, kpoints=kpoints)


two_pi = 2.0 * math.pi


def integrate_all(orbitals, potential, batch_pairs):
    per_turn = 16
    turns = BATCHES // per_turn

    def advance(pair_table, turn):
        start = (turn * per_turn).astype(jnp.int32)
        values = lax.dynamic_slice_in_dim(orbitals, start, per_turn, 0)
        weights = lax.dynamic_slice_in_dim(potential, start, per_turn, 0)
        targets = lax.dynamic_slice_in_dim(batch_pairs, start, per_turn, 0)
        scaled = (values.astype(jnp.float32) * weights[:, None, None, :]).astype(jnp.bfloat16)
        blocks = jnp.einsum("gxap,gybp->xygab", values.astype(jnp.float32), scaled.astype(jnp.float32), precision=lax.Precision.HIGHEST)
        blocks = blocks.reshape(NAO * NAO, per_turn * ABAT * ABAT)
        return pair_table.at[:, targets.reshape(-1)].add(blocks), None

    empty = jnp.zeros((NAO * NAO, NPAIR), jnp.float32)
    pair_table, _ = lax.scan(advance, empty, jnp.arange(turns, dtype=jnp.int32))
    return pair_table


def flip_blocks(blocks):
    return blocks.reshape(NAO, NAO, -1).transpose(1, 0, 2).reshape(NAO * NAO, -1)


def reference(orbitals, potential, batch_pairs, pair_info, mirror, cell_table, kpoints):
    pair_table = integrate_all(orbitals, potential, batch_pairs)
    symmetric = 0.5 * (pair_table + flip_blocks(jnp.take(pair_table, mirror, axis=1)))
    cells = jnp.take(cell_table, pair_info[2], axis=0).astype(jnp.float32)
    angle = two_pi * jnp.dot(kpoints, cells.T, precision=lax.Precision.HIGHEST)

    def one_point(row_angle):
        parts = jnp.stack([symmetric * jnp.cos(row_angle)[None, :], symmetric * jnp.sin(row_angle)[None, :]])
        parts = parts.reshape(2, NAO, NAO, NPAIR).transpose(0, 3, 1, 2)
        dense = jnp.zeros((2, ATOMS, ATOMS, NAO, NAO), jnp.float32).at[:, pair_info[0], pair_info[1]].add(parts)
        return dense.transpose(0, 1, 3, 2, 4).reshape(2, ATOMS, NAO, ATOMS * NAO)

    return lax.map(one_point, angle)
```

```python
import functools
import math

import jax
import jax.numpy as jnp
from jax import lax
from jax.experimental import pallas as pl
from jax.experimental.pallas import tpu as pltpu
from jax.sharding import PartitionSpec as P

NAO = 13
XP = 16
HALF = 7
CP = 64
ATOM_DEV = 4
A_STEP = 8

two_pi = 2.0 * math.pi
NT = (((1,), (1,)), ((), ()))


def integrate_kernel(ids_ref, orb_ref, pot_ref, pairs_ref, out_ref, rows_f32, left, right, codes, acc):
    step = pl.program_id(0)
    _, width, slots, points = orb_ref.shape

    @pl.when(step == 0)
    def _():
        rows_f32[...] = jnp.zeros_like(rows_f32)
        right[...] = jnp.zeros_like(right)
        codes[...] = jnp.full_like(codes, -1)
        acc[...] = jnp.zeros_like(acc)

    weight = pot_ref[0]
    for y in range(width):
        vals = orb_ref[0, y].astype(jnp.float32)
        base = (y % HALF) * 128 + (y // HALF) * CP
        right[base : base + slots, :] = (vals * weight).astype(jnp.bfloat16)
        rows_f32[y * slots : (y + 1) * slots, :] = vals
    for a in range(slots):
        left[a * XP : (a + 1) * XP, :] = rows_f32[pl.ds(a, XP, stride=slots), :].astype(jnp.bfloat16)
    pairs = pairs_ref[0]
    codes[:, 0:slots] = pairs * 2
    codes[:, CP : CP + slots] = pairs * 2 + 1
    ids = ids_ref[...]
    for a0 in range(0, slots, A_STEP):
        prod = lax.dot_general(
            left[a0 * XP : (a0 + A_STEP) * XP, :], right[...], NT, preferred_element_type=jnp.float32
        )
        high = prod.astype(jnp.bfloat16)
        low = (prod - high.astype(jnp.float32)).astype(jnp.bfloat16)
        cols, hots = [], []
        for a in range(A_STEP):
            parts = [
                part[a * XP : (a + 1) * XP, yp * 128 : (yp + 1) * 128]
                for part in (high, low)
                for yp in range(HALF)
            ]
            cols.append(jnp.concatenate(parts, axis=0))
            hots.append(
                (codes[a0 + a : a0 + a + 1, :] == ids).astype(jnp.float32).astype(jnp.bfloat16)
            )
        acc[...] += lax.dot_general(
            jnp.concatenate(cols, axis=1),
            jnp.concatenate(hots, axis=1),
            NT,
            preferred_element_type=jnp.float32,
        )

    @pl.when(step == pl.num_programs(0) - 1)
    def _():
        half = HALF * XP
        out_ref[...] = acc[:half, :] + acc[half:, :]


def integrate(ids, orbitals, potential, batch_pairs):
    count, width, slots, points = orbitals.shape
    ncol = ids.shape[0]
    return pl.pallas_call(
        integrate_kernel,
        grid=(count,),
        out_shape=jax.ShapeDtypeStruct((HALF * XP, ncol), jnp.float32),
        in_specs=[
            pl.BlockSpec((ncol, 128), lambda b: (0, 0)),
            pl.BlockSpec((1, width, slots, points), lambda b: (b, 0, 0, 0)),
            pl.BlockSpec((1, 1, points), lambda b: (b, 0, 0)),
            pl.BlockSpec((1, slots, slots), lambda b: (b, 0, 0)),
        ],
        out_specs=pl.BlockSpec((HALF * XP, ncol), lambda b: (0, 0)),
        scratch_shapes=[
            pltpu.VMEM((XP * slots, points), jnp.float32),
            pltpu.VMEM((slots * XP, points), jnp.bfloat16),
            pltpu.VMEM((HALF * 128, points), jnp.bfloat16),
            pltpu.VMEM((slots, 128), jnp.int32),
            pltpu.VMEM((2 * HALF * XP, ncol), jnp.float32),
        ],
        compiler_params=pltpu.CompilerParams(
            dimension_semantics=("arbitrary",), vmem_limit_bytes=48 * 1024 * 1024
        ),
    )(ids, orbitals, potential.reshape(count, 1, points), batch_pairs)


def phase_sum(blocks, info, cell_table, kpoints, first_atom, atoms):
    cells = jnp.take(cell_table, info[2], axis=0).astype(jnp.float32)
    angle = two_pi * jnp.dot(kpoints, cells.T, precision=lax.Precision.HIGHEST)
    phases = jnp.stack([jnp.cos(angle), jnp.sin(angle)], axis=1)
    row_hot = (
        info[0][:, None] - first_atom == jnp.arange(ATOM_DEV, dtype=jnp.int32)[None, :]
    ).astype(jnp.float32)
    col_hot = (info[1][:, None] == jnp.arange(atoms, dtype=jnp.int32)[None, :]).astype(jnp.float32)
    shaped = blocks.reshape(NAO, NAO, -1)
    weighted = jnp.einsum(
        "ksp,abp,pi->ksiabp", phases, shaped, row_hot, precision=lax.Precision.HIGHEST
    )
    dense = jnp.einsum("ksiabp,pj->ksiajb", weighted, col_hot, precision=lax.Precision.HIGHEST)
    return dense.reshape(kpoints.shape[0], 2, ATOM_DEV, NAO, atoms * NAO)


def on_device(orbitals, potential, batch_pairs, pair_info, mirror, cell_table, kpoints):
    grid_count = lax.axis_size("grid")
    kpt_count = lax.axis_size("kpt")
    npairs = pair_info.shape[1]
    pair_dev = npairs // (grid_count * kpt_count)
    row_pairs = pair_dev // grid_count
    grid_pos = lax.axis_index("grid")
    kpt_pos = lax.axis_index("kpt")
    half = grid_count // 2

    shift = jnp.arange(-1, 2, dtype=jnp.int32)[:, None]
    slot = jnp.arange(pair_dev, dtype=jnp.int32)[None, :]

    def pair_id(offset):
        holder = (grid_pos + shift + offset + grid_count) % grid_count
        return (holder * kpt_count + kpt_pos) * pair_dev + slot

    ids = jnp.stack([pair_id(0), jnp.take(mirror, pair_id(half))])
    ids = ids[:, :, None, :] * 2 + jnp.arange(2, dtype=jnp.int32)[None, None, :, None]
    ids = jnp.broadcast_to(ids.reshape(-1, 1), (12 * pair_dev, 128))
    table = integrate(ids, orbitals, potential, batch_pairs)
    table = table.reshape(HALF, XP, 2, 3, 2, grid_count, row_pairs)[:, :NAO]
    send = table.transpose(5, 2, 3, 6, 4, 0, 1)
    got = lax.all_to_all(send, "grid", split_axis=0, concat_axis=0, tiled=True)
    direct = sum(jnp.roll(got[:, 0, s], s - 1, axis=0) for s in range(3))
    mirrored = sum(jnp.roll(got[:, 1, s], s - 1 + half, axis=0) for s in range(3))

    def square(value):
        return value.reshape(grid_count, row_pairs, 2 * HALF, NAO)[:, :, :NAO]

    sym = 0.5 * (square(direct).transpose(3, 2, 0, 1) + square(mirrored).transpose(2, 3, 0, 1))
    gathered = lax.all_gather(sym.reshape(NAO * NAO, 1, -1), "kpt", axis=1, tiled=True)
    info = pair_info.reshape(3, grid_count, kpt_count, grid_count, row_pairs)
    info = lax.dynamic_slice_in_dim(info, grid_pos, 1, 3)[:, :, :, 0]
    info = info.transpose(0, 2, 1, 3).reshape(3, -1)
    atoms = ATOM_DEV * grid_count
    return phase_sum(
        gathered.reshape(NAO * NAO, -1), info, cell_table, kpoints, grid_pos * ATOM_DEV, atoms
    )


def solution(mesh):
    return jax.shard_map(
        on_device,
        mesh=mesh,
        in_specs=(
            P(("grid", "kpt"), None, None, None),
            P(("grid", "kpt"), None),
            P(("grid", "kpt"), None, None),
            P(),
            P(),
            P(),
            P("kpt", None),
        ),
        out_specs=P("kpt", None, "grid", None, None),
        check_vma=False,
    )
```

```python
import functools
import math

import jax
import jax.numpy as jnp
from jax import lax
from jax.experimental import pallas as pl
from jax.experimental.pallas import tpu as pltpu
from jax.sharding import PartitionSpec as P

NAO = 13
XP = 16
HALF = 7
CP = 64
ATOM_DEV = 4
A_STEP = 8

two_pi = 2.0 * math.pi
MESH = pl.DeviceIdType.MESH
NT = (((1,), (1,)), ((), ()))


def integrate_kernel(
    ids_ref, orb_ref, pot_ref, pairs_ref, out_ref, rows_f32, left, right, codes, acc, turned
):
    step = pl.program_id(0)
    _, width, slots, points = orb_ref.shape

    @pl.when(step == 0)
    def _():
        rows_f32[...] = jnp.zeros_like(rows_f32)
        right[...] = jnp.zeros_like(right)
        codes[...] = jnp.full_like(codes, -1)
        acc[...] = jnp.zeros_like(acc)

    weight = pot_ref[0]
    for y in range(width):
        vals = orb_ref[0, y].astype(jnp.float32)
        base = (y % HALF) * 128 + (y // HALF) * CP
        right[base : base + slots, :] = (vals * weight).astype(jnp.bfloat16)
        rows_f32[y * slots : (y + 1) * slots, :] = vals
    for a in range(slots):
        left[a * XP : (a + 1) * XP, :] = rows_f32[pl.ds(a, XP, stride=slots), :].astype(jnp.bfloat16)
    pairs = pairs_ref[0]
    codes[:, 0:slots] = pairs * 2
    codes[:, CP : CP + slots] = pairs * 2 + 1
    ids = ids_ref[...]
    for a0 in range(0, slots, A_STEP):
        prod = lax.dot_general(
            left[a0 * XP : (a0 + A_STEP) * XP, :], right[...], NT, preferred_element_type=jnp.float32
        )
        high = prod.astype(jnp.bfloat16)
        low = (prod - high.astype(jnp.float32)).astype(jnp.bfloat16)
        cols, hots = [], []
        for a in range(A_STEP):
            parts = [
                part[a * XP : (a + 1) * XP, yp * 128 : (yp + 1) * 128]
                for part in (high, low)
                for yp in range(HALF)
            ]
            cols.append(jnp.concatenate(parts, axis=0))
            hots.append(
                (codes[a0 + a : a0 + a + 1, :] == ids).astype(jnp.float32).astype(jnp.bfloat16)
            )
        acc[...] += lax.dot_general(
            jnp.concatenate(cols, axis=1),
            jnp.concatenate(hots, axis=1),
            NT,
            preferred_element_type=jnp.float32,
        )

    @pl.when(step == pl.num_programs(0) - 1)
    def _():
        half = HALF * XP
        out_ref[...] = jnp.zeros_like(out_ref)
        turned[:, 0:half] = jnp.transpose(acc[:half, :] + acc[half:, :])
        pair_dev = out_ref.shape[0]
        for q in range(pair_dev):
            out_ref[q, 0:12, 0:half] = turned[pl.ds(q, 12, stride=pair_dev), 0:half]


def integrate(ids, orbitals, potential, batch_pairs):
    count, width, slots, points = orbitals.shape
    ncol = ids.shape[0]
    return pl.pallas_call(
        integrate_kernel,
        grid=(count,),
        out_shape=jax.ShapeDtypeStruct((ncol // 12, XP, 128), jnp.float32),
        in_specs=[
            pl.BlockSpec((ncol, 128), lambda b: (0, 0)),
            pl.BlockSpec((1, width, slots, points), lambda b: (b, 0, 0, 0)),
            pl.BlockSpec((1, 1, points), lambda b: (b, 0, 0)),
            pl.BlockSpec((1, slots, slots), lambda b: (b, 0, 0)),
        ],
        out_specs=pl.BlockSpec((ncol // 12, XP, 128), lambda b: (0, 0, 0)),
        scratch_shapes=[
            pltpu.VMEM((XP * slots, points), jnp.float32),
            pltpu.VMEM((slots * XP, points), jnp.bfloat16),
            pltpu.VMEM((HALF * 128, points), jnp.bfloat16),
            pltpu.VMEM((slots, 128), jnp.int32),
            pltpu.VMEM((2 * HALF * XP, ncol), jnp.float32),
            pltpu.VMEM((ncol, 128), jnp.float32),
        ],
        compiler_params=pltpu.CompilerParams(
            dimension_semantics=("arbitrary",), vmem_limit_bytes=48 * 1024 * 1024
        ),
    )(ids, orbitals, potential.reshape(count, 1, points), batch_pairs)


def exchange_kernel(
    grid_count, kpt_count, send_ref, info_ref, cells_ref, kpt_ref, out_ref,
    landed, shared, turned, flipped, hot, phase, send1, recv1, send2, recv2,
):
    g = lax.axis_index("grid")
    k = lax.axis_index("kpt")
    barrier = pltpu.get_barrier_semaphore()

    def grid_peer(d):
        return (lax.rem(g + d, grid_count), k)

    def kpt_peer(d):
        return (g, lax.rem(k + d, kpt_count))

    for d in range(1, grid_count):
        pl.semaphore_signal(barrier, inc=1, device_id=grid_peer(d), device_id_type=MESH)
    for d in range(1, kpt_count):
        pl.semaphore_signal(barrier, inc=1, device_id=kpt_peer(d), device_id_type=MESH)
    pl.semaphore_wait(barrier, grid_count + kpt_count - 2)

    outgoing = []
    for d in range(1, grid_count):
        peer = grid_peer(d)
        copy = pltpu.make_async_remote_copy(
            src_ref=send_ref.at[peer[0]],
            dst_ref=landed.at[pl.ds(pl.multiple_of(g * XP, XP), XP), :],
            send_sem=send1.at[d],
            recv_sem=recv1.at[d],
            device_id=peer,
            device_id_type=MESH,
        )
        copy.start()
        outgoing.append(copy)
    landed[pl.ds(pl.multiple_of(g * XP, XP), XP), :] = send_ref[g]

    pairs = grid_count * kpt_count
    lanes = NAO * pairs
    atoms = ATOM_DEV * grid_count
    total = info_ref.shape[1]
    pair = lax.broadcasted_iota(jnp.int32, (total, pairs), 1)
    source = ((pair % grid_count) * kpt_count + pair // grid_count) * grid_count + g
    pick = (lax.broadcasted_iota(jnp.int32, (total, pairs), 0) == source).astype(jnp.float32)
    info = jnp.dot(
        info_ref[...].astype(jnp.float32).astype(jnp.bfloat16),
        pick.astype(jnp.bfloat16),
        preferred_element_type=jnp.float32,
    )
    lane = lax.broadcasted_iota(jnp.int32, (pairs, lanes), 1)
    spread = (lane % pairs == lax.broadcasted_iota(jnp.int32, (pairs, lanes), 0)).astype(jnp.float32)
    info = jnp.dot(
        info.astype(jnp.bfloat16), spread.astype(jnp.bfloat16), preferred_element_type=jnp.float32
    ).astype(jnp.int32)
    first, second, cell = info[0:1], info[1:2], info[2:3]
    angle = two_pi * jnp.sum(cells_ref[...].astype(jnp.float32) * kpt_ref[...], axis=1, keepdims=True)
    at_cell = lax.broadcasted_iota(jnp.int32, (cells_ref.shape[0], lanes), 0) == cell
    for part, values in enumerate((jnp.cos(angle), jnp.sin(angle))):
        row = jnp.sum(jnp.where(at_cell, values, 0.0), axis=0, keepdims=True)
        for i in range(ATOM_DEV):
            at = part * ATOM_DEV + i
            phase[at : at + 1, :] = jnp.where(first == g * ATOM_DEV + i, row, 0.0)
    chunk = XP * NAO
    for top in range(0, atoms * NAO, chunk):
        row = lax.broadcasted_iota(jnp.int32, (chunk, lanes), 0)
        atom = (row * 20165) // 262144
        orbital = row - atom * NAO
        match = lax.broadcasted_iota(jnp.int32, (chunk, lanes), 1) // pairs == orbital
        match = match & (atom + top // NAO == second)
        hot[top : top + chunk, :] = match.astype(jnp.float32).astype(jnp.bfloat16)

    for copy in outgoing:
        copy.wait()
    half = grid_count // 2
    for kind in range(2):
        for par in range(2):
            value = None
            for s in range(3):
                part = landed[pl.ds(kind * 6 + s * 2 + par, grid_count, stride=XP), :]
                turn = (s - 1 + kind * half) % grid_count
                if turn:
                    part = pltpu.roll(part, turn, 0)
                value = part if value is None else value + part
            base = (kind * 2 + par) * grid_count
            shared[k, base : base + grid_count, :] = value

    outgoing = []
    for d in range(1, kpt_count):
        copy = pltpu.make_async_remote_copy(
            src_ref=shared.at[k],
            dst_ref=shared.at[k],
            send_sem=send2.at[d],
            recv_sem=recv2.at[d],
            device_id=kpt_peer(d),
            device_id_type=MESH,
        )
        copy.start()
        outgoing.append(copy)
    for copy in outgoing:
        copy.wait()

    width = min(2 * pairs, 128)
    chunks = 2 * pairs // width
    for kp in range(2):
        block = jnp.concatenate(
            [shared[c, kp * 2 * grid_count + par * grid_count : kp * 2 * grid_count + (par + 1) * grid_count, :]
             for par in range(2) for c in range(kpt_count)],
            axis=0,
        )
        block = jnp.transpose(block)
        for t in range(chunks):
            turned[kp * chunks + t] = block[:, t * width : (t + 1) * width]

    def half_lanes(kind, par, rows):
        if pairs < width:
            return turned[kind, rows, :][:, par * pairs : (par + 1) * pairs]
        parts = range(par * pairs // width, (par + 1) * pairs // width)
        return jnp.concatenate([turned[kind * chunks + t, rows, :] for t in parts], axis=1)

    flipped[...] = jnp.zeros_like(flipped)
    for x in range(NAO):
        for par in range(2):
            flipped[par * HALF : (par + 1) * HALF, x * pairs : (x + 1) * pairs] = half_lanes(
                1, par, pl.ds(x, HALF, stride=XP)
            )
    direct = jnp.concatenate(
        [half_lanes(0, y // HALF, pl.ds((y % HALF) * XP, XP)) for y in range(NAO)], axis=1
    )
    sym = 0.5 * (direct + flipped[...])
    rows = jnp.concatenate([sym * phase[at : at + 1, :] for at in range(2 * ATOM_DEV)], axis=0)
    high = rows.astype(jnp.bfloat16)
    low = (rows - high.astype(jnp.float32)).astype(jnp.bfloat16)
    dense = lax.dot_general(
        jnp.concatenate([high, low], axis=0), hot[...], NT, preferred_element_type=jnp.float32
    )
    count = 2 * ATOM_DEV * XP
    dense = dense[:count] + dense[count:]
    for at in range(2 * ATOM_DEV):
        out_ref[0, at // ATOM_DEV, at % ATOM_DEV] = dense[at * XP : at * XP + NAO, :]


def exchange(send, pair_info, cell_table, kpoints, grid_count, kpt_count):
    pairs = grid_count * kpt_count
    lanes = NAO * pairs
    atoms = ATOM_DEV * grid_count
    width = min(2 * pairs, 128)
    chunks = 2 * pairs // width
    vmem = pl.BlockSpec(memory_space=pltpu.VMEM)
    return pl.pallas_call(
        functools.partial(exchange_kernel, grid_count, kpt_count),
        out_shape=jax.ShapeDtypeStruct((1, 2, ATOM_DEV, NAO, atoms * NAO), jnp.float32),
        in_specs=[vmem] * 4,
        out_specs=vmem,
        scratch_shapes=[
            pltpu.VMEM((grid_count * XP, 128), jnp.float32),
            pltpu.VMEM((kpt_count, 4 * grid_count, 128), jnp.float32),
            pltpu.VMEM((2 * chunks, 128, width), jnp.float32),
            pltpu.VMEM((XP, lanes), jnp.float32),
            pltpu.VMEM((atoms * NAO, lanes), jnp.bfloat16),
            pltpu.VMEM((2 * ATOM_DEV, lanes), jnp.float32),
            pltpu.SemaphoreType.DMA((grid_count,)),
            pltpu.SemaphoreType.DMA((grid_count,)),
            pltpu.SemaphoreType.DMA((kpt_count,)),
            pltpu.SemaphoreType.DMA((kpt_count,)),
        ],
        compiler_params=pltpu.CompilerParams(
            collective_id=0, has_side_effects=True, vmem_limit_bytes=56 * 1024 * 1024
        ),
    )(send, pair_info, cell_table, kpoints)


def on_device(orbitals, potential, batch_pairs, pair_info, mirror, cell_table, kpoints):
    grid_count = lax.axis_size("grid")
    kpt_count = lax.axis_size("kpt")
    npairs = pair_info.shape[1]
    pair_dev = npairs // (grid_count * kpt_count)
    assert pair_dev == grid_count
    grid_pos = lax.axis_index("grid")
    kpt_pos = lax.axis_index("kpt")
    half = grid_count // 2

    shift = jnp.arange(-1, 2, dtype=jnp.int32)[:, None]
    slot = jnp.arange(pair_dev, dtype=jnp.int32)[None, :]

    def pair_id(offset):
        holder = (grid_pos + shift + offset + grid_count) % grid_count
        return (holder * kpt_count + kpt_pos) * pair_dev + slot

    ids = jnp.stack([pair_id(0), jnp.take(mirror, pair_id(half))])
    ids = ids[:, :, None, :] * 2 + jnp.arange(2, dtype=jnp.int32)[None, None, :, None]
    ids = jnp.broadcast_to(ids.reshape(-1, 1), (12 * pair_dev, 128))
    send = integrate(ids, orbitals, potential, batch_pairs)
    return exchange(send, pair_info, cell_table, kpoints, grid_count, kpt_count)


def solution(mesh):
    return jax.shard_map(
        on_device,
        mesh=mesh,
        in_specs=(
            P(("grid", "kpt"), None, None, None),
            P(("grid", "kpt"), None),
            P(("grid", "kpt"), None, None),
            P(),
            P(),
            P(),
            P("kpt", None),
        ),
        out_specs=P("kpt", None, "grid", None, None),
        check_vma=False,
    )
```

```python
import functools
import math

import jax
import jax.numpy as jnp
from jax import lax
from jax.experimental import pallas as pl
from jax.experimental.pallas import tpu as pltpu
from jax.sharding import PartitionSpec as P

NAO = 13
XP = 16
HALF = 7
CP = 64
ATOM_DEV = 4
A_STEP = 8

two_pi = 2.0 * math.pi
MESH = pl.DeviceIdType.MESH
NT = (((1,), (1,)), ((), ()))


def integrate_kernel(
    grid_count, kpt_count, orb_ref, pot_ref, pairs_ref, mirror_ref, out_ref,
    rows_f32, left, right, codes, ids, acc, turned,
):
    step = pl.program_id(0)
    _, width, slots, points = orb_ref.shape
    pair_dev = out_ref.shape[0]
    g = lax.axis_index("grid")
    k = lax.axis_index("kpt")

    def first_pair(offset):
        return (lax.rem(g + offset + grid_count, grid_count) * kpt_count + k) * pair_dev

    @pl.when(step == 0)
    def _():
        rows_f32[...] = jnp.zeros_like(rows_f32)
        right[...] = jnp.zeros_like(right)
        codes[...] = jnp.full_like(codes, -1)
        acc[...] = jnp.zeros_like(acc)
        slot = lax.broadcasted_iota(jnp.int32, (pair_dev, 128), 0)
        for s in range(3):
            for par in range(2):
                at = (s * 2 + par) * pair_dev
                ids[at : at + pair_dev, :] = (slot + first_pair(s - 1)) * 2 + par

    weight = pot_ref[0]
    for y in range(width):
        vals = orb_ref[0, y].astype(jnp.float32)
        base = (y % HALF) * 128 + (y // HALF) * CP
        right[base : base + slots, :] = (vals * weight).astype(jnp.bfloat16)
        rows_f32[y * slots : (y + 1) * slots, :] = vals
    for a in range(slots):
        left[a * XP : (a + 1) * XP, :] = rows_f32[pl.ds(a, XP, stride=slots), :].astype(jnp.bfloat16)
    pairs = pairs_ref[0]
    codes[:, 0:slots] = pairs * 2
    codes[:, CP : CP + slots] = pairs * 2 + 1
    wanted = ids[...]
    for a0 in range(0, slots, A_STEP):
        prod = lax.dot_general(
            left[a0 * XP : (a0 + A_STEP) * XP, :], right[...], NT, preferred_element_type=jnp.float32
        )
        high = prod.astype(jnp.bfloat16)
        low = (prod - high.astype(jnp.float32)).astype(jnp.bfloat16)
        cols, hots = [], []
        for a in range(A_STEP):
            parts = [
                part[a * XP : (a + 1) * XP, yp * 128 : (yp + 1) * 128]
                for part in (high, low)
                for yp in range(HALF)
            ]
            cols.append(jnp.concatenate(parts, axis=0))
            hots.append(
                (codes[a0 + a : a0 + a + 1, :] == wanted).astype(jnp.float32).astype(jnp.bfloat16)
            )
        acc[...] += lax.dot_general(
            jnp.concatenate(hots, axis=1),
            jnp.concatenate(cols, axis=1),
            NT,
            preferred_element_type=jnp.float32,
        )

    @pl.when(step == pl.num_programs(0) - 1)
    def _():
        half = HALF * XP
        out_ref[...] = jnp.zeros_like(out_ref)
        table = acc[:, :half] + acc[:, half:]
        count = 6 * pair_dev
        turned[0:count, 0:half] = table
        npairs = mirror_ref.shape[1]
        every = lax.broadcasted_iota(jnp.int32, (pair_dev, npairs), 1)
        row = lax.broadcasted_iota(jnp.int32, (pair_dev, npairs), 0)
        partner = mirror_ref[...].astype(jnp.float32)
        col = lax.broadcasted_iota(jnp.int32, (pair_dev, pair_dev), 1)
        for s in range(3):
            at_pair = every == row + first_pair(s - 1 + grid_count // 2)
            source = jnp.sum(jnp.where(at_pair, partner, 0.0), axis=1, keepdims=True)
            swap = (source == (col + first_pair(s - 1)).astype(jnp.float32)).astype(jnp.float32)
            for par in range(2):
                at = (s * 2 + par) * pair_dev
                turned[count + at : count + at + pair_dev, 0:half] = jnp.dot(
                    swap,
                    table[at : at + pair_dev, :],
                    precision=lax.Precision.HIGHEST,
                    preferred_element_type=jnp.float32,
                )
        for q in range(pair_dev):
            out_ref[q, 0:12, 0:half] = turned[pl.ds(q, 12, stride=pair_dev), 0:half]


def integrate(orbitals, potential, batch_pairs, mirror, grid_count, kpt_count, pair_dev):
    count, width, slots, points = orbitals.shape
    return pl.pallas_call(
        functools.partial(integrate_kernel, grid_count, kpt_count),
        grid=(count,),
        out_shape=jax.ShapeDtypeStruct((pair_dev, XP, 128), jnp.float32),
        in_specs=[
            pl.BlockSpec((1, width, slots, points), lambda b: (b, 0, 0, 0)),
            pl.BlockSpec((1, 1, points), lambda b: (b, 0, 0)),
            pl.BlockSpec((1, slots, slots), lambda b: (b, 0, 0)),
            pl.BlockSpec((1, mirror.shape[0]), lambda b: (0, 0)),
        ],
        out_specs=pl.BlockSpec((pair_dev, XP, 128), lambda b: (0, 0, 0)),
        scratch_shapes=[
            pltpu.VMEM((XP * slots, points), jnp.float32),
            pltpu.VMEM((slots * XP, points), jnp.bfloat16),
            pltpu.VMEM((HALF * 128, points), jnp.bfloat16),
            pltpu.VMEM((slots, 128), jnp.int32),
            pltpu.VMEM((6 * pair_dev, 128), jnp.int32),
            pltpu.VMEM((6 * pair_dev, 2 * HALF * XP), jnp.float32),
            pltpu.VMEM((12 * pair_dev, 128), jnp.float32),
        ],
        compiler_params=pltpu.CompilerParams(
            dimension_semantics=("arbitrary",), vmem_limit_bytes=48 * 1024 * 1024
        ),
    )(orbitals, potential.reshape(count, 1, points), batch_pairs, mirror.reshape(1, -1))


def exchange_kernel(
    grid_count, kpt_count, send_ref, info_ref, cells_ref, kpt_ref, out_ref,
    landed, shared, turned, flipped, hot, phase, send1, recv1, send2, recv2,
):
    g = lax.axis_index("grid")
    k = lax.axis_index("kpt")
    barrier = pltpu.get_barrier_semaphore()

    def grid_peer(d):
        return (lax.rem(g + d, grid_count), k)

    def kpt_peer(d):
        return (g, lax.rem(k + d, kpt_count))

    for d in range(1, grid_count):
        pl.semaphore_signal(barrier, inc=1, device_id=grid_peer(d), device_id_type=MESH)
    for d in range(1, kpt_count):
        pl.semaphore_signal(barrier, inc=1, device_id=kpt_peer(d), device_id_type=MESH)
    pairs = grid_count * kpt_count
    lanes = NAO * pairs
    atoms = ATOM_DEV * grid_count
    total = info_ref.shape[1]
    pair = lax.broadcasted_iota(jnp.int32, (1, pairs), 1)
    source = ((pair % grid_count) * kpt_count + pair // grid_count) * grid_count + g
    pick = (lax.broadcasted_iota(jnp.int32, (total, pairs), 0) == source).astype(jnp.float32)
    info = jnp.dot(
        info_ref[...].astype(jnp.float32).astype(jnp.bfloat16),
        pick.astype(jnp.bfloat16),
        preferred_element_type=jnp.float32,
    )
    lane = lax.broadcasted_iota(jnp.int32, (1, lanes), 1)
    lane_orbital = lane // pairs
    lane_pair = lane - lane_orbital * pairs
    spread = (lane_pair == lax.broadcasted_iota(jnp.int32, (pairs, lanes), 0)).astype(jnp.float32)
    info = jnp.dot(
        info.astype(jnp.bfloat16), spread.astype(jnp.bfloat16), preferred_element_type=jnp.float32
    ).astype(jnp.int32)
    first, second, cell = info[0:1], info[1:2], info[2:3]
    vectors = cells_ref[...].astype(jnp.float32)
    angle = vectors[0:1] * kpt_ref[0, 0]
    for d in range(1, 3):
        angle = angle + vectors[d : d + 1] * kpt_ref[0, d]
    angle = two_pi * angle
    at_cell = lax.broadcasted_iota(jnp.int32, (cells_ref.shape[1], lanes), 0) == cell
    values = jnp.dot(
        jnp.concatenate([jnp.cos(angle), jnp.sin(angle)], axis=0),
        at_cell.astype(jnp.float32),
        precision=lax.Precision.HIGHEST,
        preferred_element_type=jnp.float32,
    )
    for part in range(2):
        for i in range(ATOM_DEV):
            at = part * ATOM_DEV + i
            phase[at : at + 1, :] = jnp.where(
                first == g * ATOM_DEV + i, values[part : part + 1], 0.0
            )

    pl.semaphore_wait(barrier, grid_count + kpt_count - 2)

    outgoing = []
    for d in range(1, grid_count):
        peer = grid_peer(d)
        copy = pltpu.make_async_remote_copy(
            src_ref=send_ref.at[peer[0]],
            dst_ref=landed.at[pl.ds(pl.multiple_of(g * XP, XP), XP), :],
            send_sem=send1.at[d],
            recv_sem=recv1.at[d],
            device_id=peer,
            device_id_type=MESH,
        )
        copy.start()
        outgoing.append(copy)
    landed[pl.ds(pl.multiple_of(g * XP, XP), XP), :] = send_ref[g]

    chunk = XP * NAO
    target = second * NAO + lane_orbital
    row = lax.broadcasted_iota(jnp.int32, (chunk, lanes), 0)
    for top in range(0, atoms * NAO, chunk):
        hot[top : top + chunk, :] = (row == target - top).astype(jnp.float32).astype(jnp.bfloat16)

    for copy in outgoing:
        copy.wait()
    half = grid_count // 2
    for kind in range(2):
        for par in range(2):
            value = None
            for s in range(3):
                part = landed[pl.ds(kind * 6 + s * 2 + par, grid_count, stride=XP), :]
                turn = (s - 1 + kind * half) % grid_count
                if turn:
                    part = pltpu.roll(part, turn, 0)
                value = part if value is None else value + part
            base = (kind * 2 + par) * grid_count
            shared[k, base : base + grid_count, :] = value

    outgoing = []
    for d in range(1, kpt_count):
        copy = pltpu.make_async_remote_copy(
            src_ref=shared.at[k],
            dst_ref=shared.at[k],
            send_sem=send2.at[d],
            recv_sem=recv2.at[d],
            device_id=kpt_peer(d),
            device_id_type=MESH,
        )
        copy.start()
        outgoing.append(copy)
    for copy in outgoing:
        copy.wait()

    width = min(2 * pairs, 128)
    chunks = 2 * pairs // width
    for kp in range(2):
        block = jnp.concatenate(
            [shared[c, kp * 2 * grid_count + par * grid_count : kp * 2 * grid_count + (par + 1) * grid_count, :]
             for par in range(2) for c in range(kpt_count)],
            axis=0,
        )
        block = jnp.transpose(block)
        for t in range(chunks):
            turned[kp * chunks + t] = block[:, t * width : (t + 1) * width]

    def half_lanes(kind, par, rows):
        if pairs < width:
            return turned[kind, rows, :][:, par * pairs : (par + 1) * pairs]
        parts = range(par * pairs // width, (par + 1) * pairs // width)
        return jnp.concatenate([turned[kind * chunks + t, rows, :] for t in parts], axis=1)

    flipped[...] = jnp.zeros_like(flipped)
    for x in range(NAO):
        for par in range(2):
            flipped[par * HALF : (par + 1) * HALF, x * pairs : (x + 1) * pairs] = half_lanes(
                1, par, pl.ds(x, HALF, stride=XP)
            )
    direct = jnp.concatenate(
        [half_lanes(0, y // HALF, pl.ds((y % HALF) * XP, XP)) for y in range(NAO)], axis=1
    )
    sym = 0.5 * (direct + flipped[...])
    rows = jnp.concatenate([sym * phase[at : at + 1, :] for at in range(2 * ATOM_DEV)], axis=0)
    high = rows.astype(jnp.bfloat16)
    low = (rows - high.astype(jnp.float32)).astype(jnp.bfloat16)
    dense = lax.dot_general(
        jnp.concatenate([high, low], axis=0), hot[...], NT, preferred_element_type=jnp.float32
    )
    count = 2 * ATOM_DEV * XP
    dense = dense[:count] + dense[count:]
    for at in range(2 * ATOM_DEV):
        out_ref[0, at // ATOM_DEV, at % ATOM_DEV] = dense[at * XP : at * XP + NAO, :]


def exchange(send, pair_info, cell_table, kpoints, grid_count, kpt_count):
    pairs = grid_count * kpt_count
    lanes = NAO * pairs
    atoms = ATOM_DEV * grid_count
    width = min(2 * pairs, 128)
    chunks = 2 * pairs // width
    vmem = pl.BlockSpec(memory_space=pltpu.VMEM)
    return pl.pallas_call(
        functools.partial(exchange_kernel, grid_count, kpt_count),
        out_shape=jax.ShapeDtypeStruct((1, 2, ATOM_DEV, NAO, atoms * NAO), jnp.float32),
        in_specs=[vmem, vmem, vmem, pl.BlockSpec(memory_space=pltpu.SMEM)],
        out_specs=vmem,
        scratch_shapes=[
            pltpu.VMEM((grid_count * XP, 128), jnp.float32),
            pltpu.VMEM((kpt_count, 4 * grid_count, 128), jnp.float32),
            pltpu.VMEM((2 * chunks, 128, width), jnp.float32),
            pltpu.VMEM((XP, lanes), jnp.float32),
            pltpu.VMEM((atoms * NAO, lanes), jnp.bfloat16),
            pltpu.VMEM((2 * ATOM_DEV, lanes), jnp.float32),
            pltpu.SemaphoreType.DMA((grid_count,)),
            pltpu.SemaphoreType.DMA((grid_count,)),
            pltpu.SemaphoreType.DMA((kpt_count,)),
            pltpu.SemaphoreType.DMA((kpt_count,)),
        ],
        compiler_params=pltpu.CompilerParams(
            collective_id=0, has_side_effects=True, vmem_limit_bytes=56 * 1024 * 1024
        ),
    )(send, pair_info, cell_table.T, kpoints)


def on_device(orbitals, potential, batch_pairs, pair_info, mirror, cell_table, kpoints):
    grid_count = lax.axis_size("grid")
    kpt_count = lax.axis_size("kpt")
    npairs = pair_info.shape[1]
    pair_dev = npairs // (grid_count * kpt_count)
    assert pair_dev == grid_count
    send = integrate(orbitals, potential, batch_pairs, mirror, grid_count, kpt_count, pair_dev)
    return exchange(send, pair_info, cell_table, kpoints, grid_count, kpt_count)


def solution(mesh):
    return jax.shard_map(
        on_device,
        mesh=mesh,
        in_specs=(
            P(("grid", "kpt"), None, None, None),
            P(("grid", "kpt"), None),
            P(("grid", "kpt"), None, None),
            P(),
            P(),
            P(),
            P("kpt", None),
        ),
        out_specs=P("kpt", None, "grid", None, None),
        check_vma=False,
    )
```

```python
import functools
import math

import jax
import jax.numpy as jnp
from jax import lax
from jax.experimental import pallas as pl
from jax.experimental.pallas import tpu as pltpu
from jax.sharding import PartitionSpec as P

NAO = 13
XP = 16
HALF = 7
CP = 64
ATOM_DEV = 4
A_STEP = 8

two_pi = 2.0 * math.pi
MESH = pl.DeviceIdType.MESH
NT = (((1,), (1,)), ((), ()))


def whole_kernel(
    grid_count, kpt_count, orb_ref, pot_ref, pairs_ref, mirror_ref, info_ref, cells_ref, kpt_ref,
    out_ref, rows_f32, left, right, codes, ids, acc, table2, send,
    landed, shared, turned, flipped, hot, phase, send1, recv1, send2, recv2,
):
    step = pl.program_id(0)
    _, width, slots, points = orb_ref.shape
    pair_dev = send.shape[0]
    g = lax.axis_index("grid")
    k = lax.axis_index("kpt")

    def first_pair(offset):
        return (lax.rem(g + offset + grid_count, grid_count) * kpt_count + k) * pair_dev

    barrier = pltpu.get_barrier_semaphore()

    def grid_peer(d):
        return (lax.rem(g + d, grid_count), k)

    def kpt_peer(d):
        return (g, lax.rem(k + d, kpt_count))

    @pl.when(step == 0)
    def _():
        for d in range(1, grid_count):
            pl.semaphore_signal(barrier, inc=1, device_id=grid_peer(d), device_id_type=MESH)
        for d in range(1, kpt_count):
            pl.semaphore_signal(barrier, inc=1, device_id=kpt_peer(d), device_id_type=MESH)
        rows_f32[...] = jnp.zeros_like(rows_f32)
        right[...] = jnp.zeros_like(right)
        codes[...] = jnp.full_like(codes, -1)
        acc[...] = jnp.zeros_like(acc)
        slot = lax.broadcasted_iota(jnp.int32, (pair_dev, 128), 0)
        for s in range(3):
            for par in range(2):
                at = (s * 2 + par) * pair_dev
                ids[at : at + pair_dev, :] = (slot + first_pair(s - 1)) * 2 + par

    weight = pot_ref[0]
    for y in range(width):
        vals = orb_ref[0, y].astype(jnp.float32)
        base = (y % HALF) * 128 + (y // HALF) * CP
        right[base : base + slots, :] = (vals * weight).astype(jnp.bfloat16)
        rows_f32[y * slots : (y + 1) * slots, :] = vals
    for a in range(slots):
        left[a * XP : (a + 1) * XP, :] = rows_f32[pl.ds(a, XP, stride=slots), :].astype(jnp.bfloat16)
    pairs = pairs_ref[0]
    codes[:, 0:slots] = pairs * 2
    codes[:, CP : CP + slots] = pairs * 2 + 1
    wanted = ids[...]
    for a0 in range(0, slots, A_STEP):
        prod = lax.dot_general(
            left[a0 * XP : (a0 + A_STEP) * XP, :], right[...], NT, preferred_element_type=jnp.float32
        )
        high = prod.astype(jnp.bfloat16)
        low = (prod - high.astype(jnp.float32)).astype(jnp.bfloat16)
        cols, hots = [], []
        for a in range(A_STEP):
            parts = [
                part[a * XP : (a + 1) * XP, yp * 128 : (yp + 1) * 128]
                for part in (high, low)
                for yp in range(HALF)
            ]
            cols.append(jnp.concatenate(parts, axis=0))
            hots.append(
                (codes[a0 + a : a0 + a + 1, :] == wanted).astype(jnp.float32).astype(jnp.bfloat16)
            )
        acc[...] += lax.dot_general(
            jnp.concatenate(hots, axis=1),
            jnp.concatenate(cols, axis=1),
            NT,
            preferred_element_type=jnp.float32,
        )

    @pl.when(step == pl.num_programs(0) - 1)
    def _():
        half = HALF * XP
        send[...] = jnp.zeros_like(send)
        table = acc[:, :half] + acc[:, half:]
        count = 6 * pair_dev
        table2[0:count, 0:half] = table
        npairs = mirror_ref.shape[1]
        every = lax.broadcasted_iota(jnp.int32, (pair_dev, npairs), 1)
        row = lax.broadcasted_iota(jnp.int32, (pair_dev, npairs), 0)
        partner = mirror_ref[...].astype(jnp.float32)
        col = lax.broadcasted_iota(jnp.int32, (pair_dev, pair_dev), 1)
        for s in range(3):
            at_pair = every == row + first_pair(s - 1 + grid_count // 2)
            source = jnp.sum(jnp.where(at_pair, partner, 0.0), axis=1, keepdims=True)
            swap = (source == (col + first_pair(s - 1)).astype(jnp.float32)).astype(jnp.float32)
            for par in range(2):
                at = (s * 2 + par) * pair_dev
                table2[count + at : count + at + pair_dev, 0:half] = jnp.dot(
                    swap,
                    table[at : at + pair_dev, :],
                    precision=lax.Precision.HIGHEST,
                    preferred_element_type=jnp.float32,
                )
        for q in range(pair_dev):
            send[q, 0:12, 0:half] = table2[pl.ds(q, 12, stride=pair_dev), 0:half]
        pl.semaphore_wait(barrier, grid_count + kpt_count - 2)

        outgoing = []
        for d in range(1, grid_count):
            peer = grid_peer(d)
            copy = pltpu.make_async_remote_copy(
                src_ref=send.at[peer[0]],
                dst_ref=landed.at[pl.ds(pl.multiple_of(g * XP, XP), XP), :],
                send_sem=send1.at[d],
                recv_sem=recv1.at[d],
                device_id=peer,
                device_id_type=MESH,
            )
            copy.start()
            outgoing.append(copy)
        landed[pl.ds(pl.multiple_of(g * XP, XP), XP), :] = send[g]

        pairs = grid_count * kpt_count
        lanes = NAO * pairs
        atoms = ATOM_DEV * grid_count
        total = info_ref.shape[1]
        pair = lax.broadcasted_iota(jnp.int32, (1, pairs), 1)
        source = ((pair % grid_count) * kpt_count + pair // grid_count) * grid_count + g
        pick = (lax.broadcasted_iota(jnp.int32, (total, pairs), 0) == source).astype(jnp.float32)
        info = jnp.dot(
            info_ref[...].astype(jnp.float32).astype(jnp.bfloat16),
            pick.astype(jnp.bfloat16),
            preferred_element_type=jnp.float32,
        )
        lane = lax.broadcasted_iota(jnp.int32, (1, lanes), 1)
        lane_orbital = lane // pairs
        lane_pair = lane - lane_orbital * pairs
        spread = (lane_pair == lax.broadcasted_iota(jnp.int32, (pairs, lanes), 0)).astype(jnp.float32)
        info = jnp.dot(
            info.astype(jnp.bfloat16), spread.astype(jnp.bfloat16), preferred_element_type=jnp.float32
        ).astype(jnp.int32)
        first, second, cell = info[0:1], info[1:2], info[2:3]
        vectors = cells_ref[...].astype(jnp.float32)
        angle = vectors[0:1] * kpt_ref[0, 0]
        for d in range(1, 3):
            angle = angle + vectors[d : d + 1] * kpt_ref[0, d]
        angle = two_pi * angle
        at_cell = lax.broadcasted_iota(jnp.int32, (cells_ref.shape[1], lanes), 0) == cell
        values = jnp.dot(
            jnp.concatenate([jnp.cos(angle), jnp.sin(angle)], axis=0),
            at_cell.astype(jnp.float32),
            precision=lax.Precision.HIGHEST,
            preferred_element_type=jnp.float32,
        )
        for part in range(2):
            for i in range(ATOM_DEV):
                at = part * ATOM_DEV + i
                phase[at : at + 1, :] = jnp.where(
                    first == g * ATOM_DEV + i, values[part : part + 1], 0.0
                )

        chunk = XP * NAO
        target = second * NAO + lane_orbital
        row = lax.broadcasted_iota(jnp.int32, (chunk, lanes), 0)
        for top in range(0, atoms * NAO, chunk):
            hot[top : top + chunk, :] = (row == target - top).astype(jnp.float32).astype(jnp.bfloat16)

        for copy in outgoing:
            copy.wait()
        half = grid_count // 2
        for kind in range(2):
            for par in range(2):
                value = None
                for s in range(3):
                    part = landed[pl.ds(kind * 6 + s * 2 + par, grid_count, stride=XP), :]
                    turn = (s - 1 + kind * half) % grid_count
                    if turn:
                        part = pltpu.roll(part, turn, 0)
                    value = part if value is None else value + part
                base = (kind * 2 + par) * grid_count
                shared[k, base : base + grid_count, :] = value

        outgoing = []
        for d in range(1, kpt_count):
            copy = pltpu.make_async_remote_copy(
                src_ref=shared.at[k],
                dst_ref=shared.at[k],
                send_sem=send2.at[d],
                recv_sem=recv2.at[d],
                device_id=kpt_peer(d),
                device_id_type=MESH,
            )
            copy.start()
            outgoing.append(copy)
        for copy in outgoing:
            copy.wait()

        width = min(2 * pairs, 128)
        chunks = 2 * pairs // width
        for kp in range(2):
            block = jnp.concatenate(
                [shared[c, kp * 2 * grid_count + par * grid_count : kp * 2 * grid_count + (par + 1) * grid_count, :]
                 for par in range(2) for c in range(kpt_count)],
                axis=0,
            )
            block = jnp.transpose(block)
            for t in range(chunks):
                turned[kp * chunks + t] = block[:, t * width : (t + 1) * width]

        def half_lanes(kind, par, rows):
            if pairs < width:
                return turned[kind, rows, :][:, par * pairs : (par + 1) * pairs]
            parts = range(par * pairs // width, (par + 1) * pairs // width)
            return jnp.concatenate([turned[kind * chunks + t, rows, :] for t in parts], axis=1)

        flipped[...] = jnp.zeros_like(flipped)
        for x in range(NAO):
            for par in range(2):
                flipped[par * HALF : (par + 1) * HALF, x * pairs : (x + 1) * pairs] = half_lanes(
                    1, par, pl.ds(x, HALF, stride=XP)
                )
        direct = jnp.concatenate(
            [half_lanes(0, y // HALF, pl.ds((y % HALF) * XP, XP)) for y in range(NAO)], axis=1
        )
        sym = 0.5 * (direct + flipped[...])
        rows = jnp.concatenate([sym * phase[at : at + 1, :] for at in range(2 * ATOM_DEV)], axis=0)
        high = rows.astype(jnp.bfloat16)
        low = (rows - high.astype(jnp.float32)).astype(jnp.bfloat16)
        dense = lax.dot_general(
            jnp.concatenate([high, low], axis=0), hot[...], NT, preferred_element_type=jnp.float32
        )
        count = 2 * ATOM_DEV * XP
        dense = dense[:count] + dense[count:]
        for at in range(2 * ATOM_DEV):
            out_ref[0, at // ATOM_DEV, :, at % ATOM_DEV, :] = dense[at * XP : at * XP + NAO, :]


def whole(orbitals, potential, batch_pairs, mirror, pair_info, cells, kpoints, grid_count, kpt_count):
    count, width, slots, points = orbitals.shape
    pairs = grid_count * kpt_count
    pair_dev = grid_count
    lanes = NAO * pairs
    atoms = ATOM_DEV * grid_count
    lane_tile = min(2 * pairs, 128)
    return pl.pallas_call(
        functools.partial(whole_kernel, grid_count, kpt_count),
        grid=(count,),
        out_shape=jax.ShapeDtypeStruct((1, 2, NAO, ATOM_DEV, atoms * NAO), jnp.float32),
        in_specs=[
            pl.BlockSpec((1, width, slots, points), lambda b: (b, 0, 0, 0)),
            pl.BlockSpec((1, 1, points), lambda b: (b, 0, 0)),
            pl.BlockSpec((1, slots, slots), lambda b: (b, 0, 0)),
            pl.BlockSpec(mirror.shape, lambda b: (0, 0)),
            pl.BlockSpec(pair_info.shape, lambda b: (0, 0)),
            pl.BlockSpec(cells.shape, lambda b: (0, 0)),
            pl.BlockSpec(memory_space=pltpu.SMEM),
        ],
        out_specs=pl.BlockSpec((1, 2, NAO, ATOM_DEV, atoms * NAO), lambda b: (0, 0, 0, 0, 0)),
        scratch_shapes=[
            pltpu.VMEM((XP * slots, points), jnp.float32),
            pltpu.VMEM((slots * XP, points), jnp.bfloat16),
            pltpu.VMEM((HALF * 128, points), jnp.bfloat16),
            pltpu.VMEM((slots, 128), jnp.int32),
            pltpu.VMEM((6 * pair_dev, 128), jnp.int32),
            pltpu.VMEM((6 * pair_dev, 2 * HALF * XP), jnp.float32),
            pltpu.VMEM((12 * pair_dev, 128), jnp.float32),
            pltpu.VMEM((pair_dev, XP, 128), jnp.float32),
            pltpu.VMEM((grid_count * XP, 128), jnp.float32),
            pltpu.VMEM((kpt_count, 4 * grid_count, 128), jnp.float32),
            pltpu.VMEM((4 * pairs // lane_tile, 128, lane_tile), jnp.float32),
            pltpu.VMEM((XP, lanes), jnp.float32),
            pltpu.VMEM((atoms * NAO, lanes), jnp.bfloat16),
            pltpu.VMEM((2 * ATOM_DEV, lanes), jnp.float32),
            pltpu.SemaphoreType.DMA((grid_count,)),
            pltpu.SemaphoreType.DMA((grid_count,)),
            pltpu.SemaphoreType.DMA((kpt_count,)),
            pltpu.SemaphoreType.DMA((kpt_count,)),
        ],
        compiler_params=pltpu.CompilerParams(
            dimension_semantics=("arbitrary",),
            collective_id=0,
            has_side_effects=True,
            vmem_limit_bytes=60 * 1024 * 1024,
        ),
    )(orbitals, potential.reshape(count, 1, points), batch_pairs, mirror, pair_info, cells, kpoints)


def on_device(orbitals, potential, batch_pairs, pair_info, mirror, cell_table, kpoints):
    grid_count = lax.axis_size("grid")
    kpt_count = lax.axis_size("kpt")
    npairs = pair_info.shape[1]
    pair_dev = npairs // (grid_count * kpt_count)
    assert pair_dev == grid_count
    dense = whole(
        orbitals, potential, batch_pairs, mirror.reshape(1, -1), pair_info, cell_table.T, kpoints,
        grid_count, kpt_count,
    )
    return dense.transpose(0, 1, 3, 2, 4)


def solution(mesh):
    return jax.shard_map(
        on_device,
        mesh=mesh,
        in_specs=(
            P(("grid", "kpt"), None, None, None),
            P(("grid", "kpt"), None),
            P(("grid", "kpt"), None, None),
            P(),
            P(),
            P(),
            P("kpt", None),
        ),
        out_specs=P("kpt", None, "grid", None, None),
        check_vma=False,
    )
```

```python
import functools
import math

import jax
import jax.numpy as jnp
from jax import lax
from jax.experimental import pallas as pl
from jax.experimental.pallas import tpu as pltpu
from jax.sharding import PartitionSpec as P

NAO = 13
XP = 16
HALF = 7
CP = 64
ATOM_DEV = 4
A_STEP = 8
BATCH_STEP = 4

two_pi = 2.0 * math.pi
MESH = pl.DeviceIdType.MESH
NT = (((1,), (1,)), ((), ()))


def whole_kernel(
    grid_count, kpt_count, orb_ref, pot_ref, pairs_ref, mirror_ref, info_ref, cells_ref, kpt_ref,
    out_ref, rows_f32, left, right, codes, ids, acc, table2, send,
    landed, shared, turned, flipped, hot, phase, send1, recv1, send2, recv2,
):
    step = pl.program_id(0)
    _, width, slots, points = orb_ref.shape
    pair_dev = send.shape[0]
    g = lax.axis_index("grid")
    k = lax.axis_index("kpt")

    def first_pair(offset):
        return (lax.rem(g + offset + grid_count, grid_count) * kpt_count + k) * pair_dev

    barrier = pltpu.get_barrier_semaphore()

    def grid_peer(d):
        return (lax.rem(g + d, grid_count), k)

    def kpt_peer(d):
        return (g, lax.rem(k + d, kpt_count))

    @pl.when(step == 0)
    def _():
        for d in range(1, grid_count):
            pl.semaphore_signal(barrier, inc=1, device_id=grid_peer(d), device_id_type=MESH)
        for d in range(1, kpt_count):
            pl.semaphore_signal(barrier, inc=1, device_id=kpt_peer(d), device_id_type=MESH)
        rows_f32[...] = jnp.zeros_like(rows_f32)
        right[...] = jnp.zeros_like(right)
        codes[...] = jnp.full_like(codes, -1)
        acc[...] = jnp.zeros_like(acc)
        slot = lax.broadcasted_iota(jnp.int32, (pair_dev, 128), 0)
        for s in range(3):
            for par in range(2):
                at = (s * 2 + par) * pair_dev
                ids[at : at + pair_dev, :] = (slot + first_pair(s - 1)) * 2 + par

    for b in range(BATCH_STEP):
        weight = pot_ref[b]
        for y in range(width):
            vals = orb_ref[b, y].astype(jnp.float32)
            base = (y % HALF) * 128 + (y // HALF) * CP
            right[b, base : base + slots, :] = (vals * weight).astype(jnp.bfloat16)
            rows_f32[b, y * slots : (y + 1) * slots, :] = vals
        for a in range(slots):
            left[b, a * XP : (a + 1) * XP, :] = rows_f32[b, pl.ds(a, XP, stride=slots), :].astype(jnp.bfloat16)
        pairs = pairs_ref[b]
        codes[b, :, 0:slots] = pairs * 2
        codes[b, :, CP : CP + slots] = pairs * 2 + 1
        wanted = ids[...]
        for a0 in range(0, slots, A_STEP):
            prod = lax.dot_general(
                left[b, a0 * XP : (a0 + A_STEP) * XP, :], right[b], NT, preferred_element_type=jnp.float32
            )
            high = prod.astype(jnp.bfloat16)
            low = (prod - high.astype(jnp.float32)).astype(jnp.bfloat16)
            cols, hots = [], []
            for a in range(A_STEP):
                parts = [
                    part[a * XP : (a + 1) * XP, yp * 128 : (yp + 1) * 128]
                    for part in (high, low)
                    for yp in range(HALF)
                ]
                cols.append(jnp.concatenate(parts, axis=0))
                hots.append(
                    (codes[b, a0 + a : a0 + a + 1, :] == wanted).astype(jnp.float32).astype(jnp.bfloat16)
                )
            acc[...] += lax.dot_general(
                jnp.concatenate(hots, axis=1),
                jnp.concatenate(cols, axis=1),
                NT,
                preferred_element_type=jnp.float32,
            )

    @pl.when(step == pl.num_programs(0) - 1)
    def _():
        half = HALF * XP
        send[...] = jnp.zeros_like(send)
        table = acc[:, :half] + acc[:, half:]
        count = 6 * pair_dev
        table2[0:count, 0:half] = table
        npairs = mirror_ref.shape[1]
        every = lax.broadcasted_iota(jnp.int32, (pair_dev, npairs), 1)
        row = lax.broadcasted_iota(jnp.int32, (pair_dev, npairs), 0)
        partner = mirror_ref[...].astype(jnp.float32)
        col = lax.broadcasted_iota(jnp.int32, (pair_dev, pair_dev), 1)
        for s in range(3):
            at_pair = every == row + first_pair(s - 1 + grid_count // 2)
            source = jnp.sum(jnp.where(at_pair, partner, 0.0), axis=1, keepdims=True)
            swap = (source == (col + first_pair(s - 1)).astype(jnp.float32)).astype(jnp.float32)
            for par in range(2):
                at = (s * 2 + par) * pair_dev
                table2[count + at : count + at + pair_dev, 0:half] = jnp.dot(
                    swap,
                    table[at : at + pair_dev, :],
                    precision=lax.Precision.HIGHEST,
                    preferred_element_type=jnp.float32,
                )
        for q in range(pair_dev):
            send[q, 0:12, 0:half] = table2[pl.ds(q, 12, stride=pair_dev), 0:half]
        pl.semaphore_wait(barrier, grid_count + kpt_count - 2)

        outgoing = []
        for d in range(1, grid_count):
            peer = grid_peer(d)
            copy = pltpu.make_async_remote_copy(
                src_ref=send.at[peer[0]],
                dst_ref=landed.at[pl.ds(pl.multiple_of(g * XP, XP), XP), :],
                send_sem=send1.at[d],
                recv_sem=recv1.at[d],
                device_id=peer,
                device_id_type=MESH,
            )
            copy.start()
            outgoing.append(copy)
        landed[pl.ds(pl.multiple_of(g * XP, XP), XP), :] = send[g]

        pairs = grid_count * kpt_count
        lanes = NAO * pairs
        atoms = ATOM_DEV * grid_count
        total = info_ref.shape[1]
        pair = lax.broadcasted_iota(jnp.int32, (1, pairs), 1)
        source = ((pair % grid_count) * kpt_count + pair // grid_count) * grid_count + g
        pick = (lax.broadcasted_iota(jnp.int32, (total, pairs), 0) == source).astype(jnp.float32)
        info = jnp.dot(
            info_ref[...].astype(jnp.float32).astype(jnp.bfloat16),
            pick.astype(jnp.bfloat16),
            preferred_element_type=jnp.float32,
        )
        lane = lax.broadcasted_iota(jnp.int32, (1, lanes), 1)
        lane_orbital = lane // pairs
        lane_pair = lane - lane_orbital * pairs
        spread = (lane_pair == lax.broadcasted_iota(jnp.int32, (pairs, lanes), 0)).astype(jnp.float32)
        info = jnp.dot(
            info.astype(jnp.bfloat16), spread.astype(jnp.bfloat16), preferred_element_type=jnp.float32
        ).astype(jnp.int32)
        first, second, cell = info[0:1], info[1:2], info[2:3]
        vectors = cells_ref[...].astype(jnp.float32)
        angle = vectors[0:1] * kpt_ref[0, 0]
        for d in range(1, 3):
            angle = angle + vectors[d : d + 1] * kpt_ref[0, d]
        angle = two_pi * angle
        at_cell = lax.broadcasted_iota(jnp.int32, (cells_ref.shape[1], lanes), 0) == cell
        values = jnp.dot(
            jnp.concatenate([jnp.cos(angle), jnp.sin(angle)], axis=0),
            at_cell.astype(jnp.float32),
            precision=lax.Precision.HIGHEST,
            preferred_element_type=jnp.float32,
        )
        for part in range(2):
            for i in range(ATOM_DEV):
                at = part * ATOM_DEV + i
                phase[at : at + 1, :] = jnp.where(
                    first == g * ATOM_DEV + i, values[part : part + 1], 0.0
                )

        chunk = XP * NAO
        target = second * NAO + lane_orbital
        row = lax.broadcasted_iota(jnp.int32, (chunk, lanes), 0)
        for top in range(0, atoms * NAO, chunk):
            hot[top : top + chunk, :] = (row == target - top).astype(jnp.float32).astype(jnp.bfloat16)

        for copy in outgoing:
            copy.wait()
        half = grid_count // 2
        for kind in range(2):
            for par in range(2):
                value = None
                for s in range(3):
                    part = landed[pl.ds(kind * 6 + s * 2 + par, grid_count, stride=XP), :]
                    turn = (s - 1 + kind * half) % grid_count
                    if turn:
                        part = pltpu.roll(part, turn, 0)
                    value = part if value is None else value + part
                base = (kind * 2 + par) * grid_count
                shared[k, base : base + grid_count, :] = value

        outgoing = []
        for d in range(1, kpt_count):
            copy = pltpu.make_async_remote_copy(
                src_ref=shared.at[k],
                dst_ref=shared.at[k],
                send_sem=send2.at[d],
                recv_sem=recv2.at[d],
                device_id=kpt_peer(d),
                device_id_type=MESH,
            )
            copy.start()
            outgoing.append(copy)
        for copy in outgoing:
            copy.wait()

        width = min(2 * pairs, 128)
        chunks = 2 * pairs // width
        for kp in range(2):
            block = jnp.concatenate(
                [shared[c, kp * 2 * grid_count + par * grid_count : kp * 2 * grid_count + (par + 1) * grid_count, :]
                 for par in range(2) for c in range(kpt_count)],
                axis=0,
            )
            block = jnp.transpose(block)
            for t in range(chunks):
                turned[kp * chunks + t] = block[:, t * width : (t + 1) * width]

        def half_lanes(kind, par, rows):
            if pairs < width:
                return turned[kind, rows, :][:, par * pairs : (par + 1) * pairs]
            parts = range(par * pairs // width, (par + 1) * pairs // width)
            return jnp.concatenate([turned[kind * chunks + t, rows, :] for t in parts], axis=1)

        flipped[...] = jnp.zeros_like(flipped)
        for x in range(NAO):
            for par in range(2):
                flipped[par * HALF : (par + 1) * HALF, x * pairs : (x + 1) * pairs] = half_lanes(
                    1, par, pl.ds(x, HALF, stride=XP)
                )
        direct = jnp.concatenate(
            [half_lanes(0, y // HALF, pl.ds((y % HALF) * XP, XP)) for y in range(NAO)], axis=1
        )
        sym = 0.5 * (direct + flipped[...])
        rows = jnp.concatenate([sym * phase[at : at + 1, :] for at in range(2 * ATOM_DEV)], axis=0)
        high = rows.astype(jnp.bfloat16)
        low = (rows - high.astype(jnp.float32)).astype(jnp.bfloat16)
        dense = lax.dot_general(
            jnp.concatenate([high, low], axis=0), hot[...], NT, preferred_element_type=jnp.float32
        )
        count = 2 * ATOM_DEV * XP
        dense = dense[:count] + dense[count:]
        for at in range(2 * ATOM_DEV):
            out_ref[0, at // ATOM_DEV, :, at % ATOM_DEV, :] = dense[at * XP : at * XP + NAO, :]


def whole(orbitals, potential, batch_pairs, mirror, pair_info, cells, kpoints, grid_count, kpt_count):
    count, width, slots, points = orbitals.shape
    pairs = grid_count * kpt_count
    pair_dev = grid_count
    lanes = NAO * pairs
    atoms = ATOM_DEV * grid_count
    lane_tile = min(2 * pairs, 128)
    return pl.pallas_call(
        functools.partial(whole_kernel, grid_count, kpt_count),
        grid=(count // BATCH_STEP,),
        out_shape=jax.ShapeDtypeStruct((1, 2, NAO, ATOM_DEV, atoms * NAO), jnp.float32),
        in_specs=[
            pl.BlockSpec((BATCH_STEP, width, slots, points), lambda b: (b, 0, 0, 0)),
            pl.BlockSpec((BATCH_STEP, 1, points), lambda b: (b, 0, 0)),
            pl.BlockSpec((BATCH_STEP, slots, slots), lambda b: (b, 0, 0)),
            pl.BlockSpec(mirror.shape, lambda b: (0, 0)),
            pl.BlockSpec(pair_info.shape, lambda b: (0, 0)),
            pl.BlockSpec(cells.shape, lambda b: (0, 0)),
            pl.BlockSpec(memory_space=pltpu.SMEM),
        ],
        out_specs=pl.BlockSpec((1, 2, NAO, ATOM_DEV, atoms * NAO), lambda b: (0, 0, 0, 0, 0)),
        scratch_shapes=[
            pltpu.VMEM((BATCH_STEP, XP * slots, points), jnp.float32),
            pltpu.VMEM((BATCH_STEP, slots * XP, points), jnp.bfloat16),
            pltpu.VMEM((BATCH_STEP, HALF * 128, points), jnp.bfloat16),
            pltpu.VMEM((BATCH_STEP, slots, 128), jnp.int32),
            pltpu.VMEM((6 * pair_dev, 128), jnp.int32),
            pltpu.VMEM((6 * pair_dev, 2 * HALF * XP), jnp.float32),
            pltpu.VMEM((12 * pair_dev, 128), jnp.float32),
            pltpu.VMEM((pair_dev, XP, 128), jnp.float32),
            pltpu.VMEM((grid_count * XP, 128), jnp.float32),
            pltpu.VMEM((kpt_count, 4 * grid_count, 128), jnp.float32),
            pltpu.VMEM((4 * pairs // lane_tile, 128, lane_tile), jnp.float32),
            pltpu.VMEM((XP, lanes), jnp.float32),
            pltpu.VMEM((atoms * NAO, lanes), jnp.bfloat16),
            pltpu.VMEM((2 * ATOM_DEV, lanes), jnp.float32),
            pltpu.SemaphoreType.DMA((grid_count,)),
            pltpu.SemaphoreType.DMA((grid_count,)),
            pltpu.SemaphoreType.DMA((kpt_count,)),
            pltpu.SemaphoreType.DMA((kpt_count,)),
        ],
        compiler_params=pltpu.CompilerParams(
            dimension_semantics=("arbitrary",),
            collective_id=0,
            has_side_effects=True,
            vmem_limit_bytes=60 * 1024 * 1024,
        ),
    )(orbitals, potential.reshape(count, 1, points), batch_pairs, mirror, pair_info, cells, kpoints)


def on_device(orbitals, potential, batch_pairs, pair_info, mirror, cell_table, kpoints):
    grid_count = lax.axis_size("grid")
    kpt_count = lax.axis_size("kpt")
    npairs = pair_info.shape[1]
    pair_dev = npairs // (grid_count * kpt_count)
    assert pair_dev == grid_count
    dense = whole(
        orbitals, potential, batch_pairs, mirror.reshape(1, -1), pair_info, cell_table.T, kpoints,
        grid_count, kpt_count,
    )
    return dense.transpose(0, 1, 3, 2, 4)


def solution(mesh):
    return jax.shard_map(
        on_device,
        mesh=mesh,
        in_specs=(
            P(("grid", "kpt"), None, None, None),
            P(("grid", "kpt"), None),
            P(("grid", "kpt"), None, None),
            P(),
            P(),
            P(),
            P("kpt", None),
        ),
        out_specs=P("kpt", None, "grid", None, None),
        check_vma=False,
    )
```
